32 devices in a mesh: row: 8 (over y, x, core), col: 4 (over z).
Axes of the slice: x: 2, y: 2, z: 4, core: 2. Of those that a mesh axis runs over, the one named last changes fastest.
Arguments:
- amplitudes: bfloat16 [4096, 3072], P(('row', 'col')), may hold values from -6 to 6
- integrals: bfloat16 [8, 3072, 9600], P('col', None, 'row'), may hold values from -0.109375 to 0.109375
- irreps: int32 [4096], P(('row', 'col')), may hold values from 0 to 7, as said below
- row_mirror: int32 [4096], P(('row', 'col')), may hold values from 0 to 127, as said below
- col_mirror: int32 [9600], replicated, may hold values from 0 to 9599, as said below
Outputs:
- symmetrized: bfloat16 [4096, 9600], P(('row', 'col'))
The draws below stay inside these ranges and needn't reach their ends.
Inputs may be any that keep to these rules, and one draw needn't show every extreme that they name: `irreps`: among the 128 pairs of one block, no irrep occurs more than 32 times; in every block one irrep, the same for all blocks, occurs exactly 32 times. A pair and its mirrored partner have the same irrep. `row_mirror`: within each block of 128 pairs the map is an involution without fixed points. `col_mirror`: an involution of the 9600 slab columns without fixed points.
All inputs are finite; a program needn't handle non-finite values.
Results may differ from the reference program's by a relative error of at most 0.0051.
Values may be sent and summed in bfloat16 or wider, within the bound.
No kernel may reach another device: no remote copies, remote signals or barrier semaphores. Data moves between devices by JAX's collectives and lax.ppermute only.
A program may use at most 192 MiB of HBM per device.

```python
import jax
import jax.numpy as jnp
from jax import lax

IRREPS = 8
KW = 3072
ROWS_DEV = 128
CAP = 32
SLAB = 9600
PAIRS = 4096


def ticket_layout(key):
    blocks = PAIRS // ROWS_DEV
    pair_count = ROWS_DEV // 2
    half_cap = CAP // 2
    base_key = jax.random.fold_in(key, 11)
    compelled_pick = jax.random.randint(jax.random.fold_in(base_key, 1), (), 0, IRREPS)
    priority_order = jax.random.permutation(jax.random.fold_in(base_key, 2), IRREPS).astype(jnp.int32)
    voucher_list = jnp.repeat(jnp.arange(IRREPS, dtype=jnp.int32), half_cap)
    voucher_count = IRREPS * half_cap

    def one_block(block_key):
        random_jitter = jax.random.randint(jax.random.fold_in(block_key, 3), (voucher_count,), 0, 65536)
        extra_reward = priority_order[voucher_list] * 16384 + jnp.where(voucher_list == compelled_pick, 262144, 0)
        merit_value = (random_jitter + extra_reward) * voucher_count + jnp.arange(voucher_count, dtype=jnp.int32)
        order = jnp.argsort(-merit_value, stable=True)
        chosen = voucher_list[order[:pair_count]]
        places = jax.random.permutation(jax.random.fold_in(block_key, 4), ROWS_DEV).astype(jnp.int32)
        first = places[0::2]
        second = places[1::2]
        labels = jnp.zeros((ROWS_DEV,), jnp.int32).at[first].set(chosen).at[second].set(chosen)
        partner = jnp.zeros((ROWS_DEV,), jnp.int32).at[first].set(second).at[second].set(first)
        return (labels, partner)
    block_keys = jax.random.split(base_key, blocks)
    labels, partner = jax.vmap(one_block)(block_keys)
    return (labels.reshape(-1), partner.reshape(-1))


def draw_irreps(key, part):
    return ticket_layout(key)[0]


def draw_row_mirror(key, part):
    return ticket_layout(key)[1]


def draw_col_mirror(key, part):
    places = jax.random.permutation(jax.random.fold_in(key, 29), SLAB).astype(jnp.int32)
    first = places[0::2]
    second = places[1::2]
    return jnp.zeros((SLAB,), jnp.int32).at[first].set(second).at[second].set(first)


def shard_levels(own_key, shape, cuts, low, high):
    level, own = 1.0, jax.random.fold_in(own_key, 6)
    for axis_at, parts in cuts:
        draws = jnp.exp(jax.random.uniform(jax.random.fold_in(own, axis_at), (parts,), jnp.float32, low / len(cuts), high / len(cuts)))
        level = level * jnp.repeat(draws, shape[axis_at] // parts).reshape([-1 if axis == axis_at else 1 for axis in range(len(shape))])
    return level


def scatter_about(rng, shape, deviation, limit, shards=(), kind=jnp.bfloat16):
    drawn = jax.random.normal(rng, shape, jnp.float32) * deviation
    if len(shards) > 0:
        drawn = shard_levels(rng, shape, shards, -0.22, 0.18) * drawn
    return jnp.clip(drawn, min=-limit, max=limit).astype(kind)


def setup_inputs(seed: int = 0) -> dict:
    key_of = jax.random.split(jax.random.key(seed), 6)
    return {
        "amplitudes": scatter_about(key_of[0], (PAIRS, KW), 1.0, 6.0, ((0, 32),)),
        "integrals": scatter_about(key_of[1], (IRREPS, KW, SLAB), KW ** -0.5, 0.109375, ((0, 4), (2, 8))),
        "irreps": draw_irreps(jax.random.fold_in(key_of[5], 71), 0),
        "row_mirror": draw_row_mirror(jax.random.fold_in(key_of[5], 71), 0),
        "col_mirror": draw_col_mirror(jax.random.fold_in(key_of[5], 71), 0),
    }


def multiply_irrep(operands):
    slot_rows, weight = operands
    return jnp.dot(slot_rows, weight, preferred_element_type=jnp.float32).astype(jnp.bfloat16)


def reference(amplitudes, integrals, irreps, row_mirror, col_mirror):
    blocks = PAIRS // ROWS_DEV
    irrep_grid = irreps.reshape(blocks, ROWS_DEV).astype(jnp.int32)
    onehot = (irrep_grid[:, :, None] == jnp.arange(IRREPS, dtype=jnp.int32)[None, None, :]).astype(jnp.int32)
    before = jnp.cumsum(onehot, axis=1) - onehot
    slot_index = jnp.sum(before * onehot, axis=2).astype(jnp.int32)
    block_ids = jnp.arange(blocks, dtype=jnp.int32)[:, None]
    position = (irrep_grid * (blocks * CAP) + block_ids * CAP + slot_index).reshape(-1).astype(jnp.int32)
    buffer = jnp.zeros((IRREPS * blocks * CAP, KW), jnp.bfloat16).at[position].set(amplitudes)
    buffer = buffer.reshape(IRREPS, blocks * CAP, KW)
    ladder_slots = lax.map(multiply_irrep, (buffer, integrals))
    ladder = ladder_slots.reshape(IRREPS * blocks * CAP, SLAB)[position]
    partner = ((jnp.arange(PAIRS, dtype=jnp.int32) // ROWS_DEV) * ROWS_DEV + row_mirror.astype(jnp.int32)).astype(jnp.int32)
    mirrored = ladder[partner][:, col_mirror.astype(jnp.int32)]
    return (ladder.astype(jnp.float32) + mirrored.astype(jnp.float32)).astype(jnp.bfloat16)
```

```python
import functools

import jax
import jax.numpy as jnp
from jax import lax
from jax.experimental import pallas as pl
from jax.experimental.pallas import tpu as pltpu
from jax.sharding import PartitionSpec as P

IRREPS = 8
F32, BF16, I32 = jnp.float32, jnp.bfloat16, jnp.int32
NN = (((1,), (0,)), ((), ()))
NT = (((1,), (1,)), ((), ()))
VMEM_LIMIT = 56 * 1024 * 1024


def iota(shape, dim):
    return lax.broadcasted_iota(I32, shape, dim)


def params():
    return pltpu.CompilerParams(vmem_limit_bytes=VMEM_LIMIT)


def pack_kernel(cols, owned, half, where_ref, irreps_ref, mirror_ref, amp_ref, slot_ref, *out_refs):
    pairs = irreps_ref.shape[1]
    square = (pairs, pairs)
    irreps = jnp.broadcast_to(irreps_ref[...], square)
    mirror = jnp.broadcast_to(mirror_ref[...], square)
    irreps_t = irreps.astype(F32).T.astype(I32)
    mirror_t = mirror.astype(F32).T.astype(I32)
    down, across = iota(square, 0), iota(square, 1)
    first = jnp.minimum(across, mirror)
    counted = (mirror_t > down) & (irreps_t == irreps) & (down < first)
    rank = jnp.sum(counted.astype(I32), axis=0, keepdims=True)
    partner = (across[:1] != first[:1]).astype(I32)
    slot = irreps_ref[...] * (2 * half) + partner * half + rank
    slot_ref[...] = slot
    rows = owned * 2 * half
    amp = amp_ref[...]
    for k in range(cols):
        base = (where_ref[1] ^ k) * rows
        onehot = (slot == base + iota((rows, pairs), 0)).astype(F32).astype(BF16)
        out_refs[k][...] = lax.dot_general(onehot, amp, NN, preferred_element_type=F32).astype(BF16)


def pack(where, irreps, mirror, amplitudes, cols, owned, half):
    pairs, contract = amplitudes.shape
    rows = owned * 2 * half
    whole = lambda shape: pl.BlockSpec(shape, lambda i, w: (0, 0))
    out = pl.pallas_call(
        functools.partial(pack_kernel, cols, owned, half),
        grid_spec=pltpu.PrefetchScalarGridSpec(
            num_scalar_prefetch=1,
            grid=(1,),
            in_specs=[whole((1, pairs)), whole((1, pairs)), whole((pairs, contract))],
            out_specs=[whole((1, pairs))] + [whole((rows, contract))] * cols,
        ),
        out_shape=[jax.ShapeDtypeStruct((1, pairs), I32)]
        + [jax.ShapeDtypeStruct((rows, contract), BF16)] * cols,
        compiler_params=params(),
        cost_estimate=pl.CostEstimate(
            flops=2 * cols * rows * pairs * contract, bytes_accessed=3 * pairs * contract * 2, transcendentals=0
        ),
        name="pack",
    )(where, irreps, mirror, amplitudes)
    return out[0], out[1:]


def product_kernel(holders, chunk_count, owned, slots, *refs):
    pieces = refs[: holders * chunk_count]
    integrals_ref = refs[holders * chunk_count]
    outs = refs[holders * chunk_count + 1 : holders * chunk_count + 1 + holders]
    rows_ref, sem = refs[-2:]
    group = chunk_count * slots

    @pl.when(pl.program_id(0) == 0)
    def _():
        copies = []
        for o in range(holders):
            for j in range(chunk_count):
                for i in range(owned):
                    n = len(copies)
                    copies.append(
                        pltpu.make_async_copy(
                            pieces[o * chunk_count + j].at[pl.ds(i * slots, slots)],
                            rows_ref.at[i, pl.ds(o * group + j * slots, slots)],
                            sem.at[n],
                        )
                    )
        for copy in copies:
            copy.start()
        for copy in copies:
            copy.wait()

    ladder = [
        lax.dot_general(rows_ref[i], integrals_ref[i], NN, preferred_element_type=F32) for i in range(owned)
    ]
    for o in range(holders):
        block = jnp.concatenate([ladder[i][o * group : (o + 1) * group] for i in range(owned)], axis=0)
        outs[o][...] = block.T.astype(BF16)


def product(pieces, integrals, holders, chunk_count, slots):
    owned, contract, share = integrals.shape
    tile = 256
    group = chunk_count * slots
    lanes = owned * group
    return pl.pallas_call(
        functools.partial(product_kernel, holders, chunk_count, owned, slots),
        grid=(pl.cdiv(share, tile),),
        in_specs=[pl.BlockSpec(memory_space=pl.ANY)] * (holders * chunk_count)
        + [pl.BlockSpec((owned, contract, tile), lambda s: (0, 0, s))],
        out_specs=[pl.BlockSpec((tile, lanes), lambda s: (s, 0))] * holders,
        out_shape=[jax.ShapeDtypeStruct((share, lanes), BF16)] * holders,
        scratch_shapes=[
            pltpu.VMEM((owned, holders * group, contract), BF16),
            pltpu.SemaphoreType.DMA((holders * chunk_count * owned,)),
        ],
        compiler_params=params(),
        cost_estimate=pl.CostEstimate(
            flops=2 * owned * holders * group * contract * share,
            bytes_accessed=2 * owned * contract * (share + holders * group),
            transcendentals=0,
        ),
        name="ladder",
    )(*pieces, integrals)


def gather_rows(mirror_ref, base, source, target, count):
    step = 16

    def some(n, carry):
        for u in range(step):
            at = n * step + u
            target[pl.ds(at, 1), :] = source[pl.ds(mirror_ref[base + at], 1), :]
        return carry

    lax.fori_loop(0, count // step, some, 0)


def symmetrize_kernel(holders, chunks, owned, half, where_ref, mirror_ref, *refs):
    parts = refs[:holders]
    outs = refs[holders : holders + len(chunks)]
    raw, wide, picked, sem = refs[holders + len(chunks) :]
    share = parts[0].shape[0]
    lanes = raw.shape[2]
    block = picked.shape[0]
    step = pl.program_id(0)

    @pl.when(step == 0)
    def _():
        copies = []
        for o in range(holders):
            copies.append(pltpu.make_async_copy(parts[o], raw.at[o], sem.at[o]))
        for copy in copies:
            copy.start()
        for o in range(holders):
            copies[o].wait()
            at = pl.multiple_of((where_ref[0] ^ o) * share, 8)
            wide[pl.ds(at, share), :] = raw[o].astype(F32)

    base = step * block
    gather_rows(mirror_ref, base, wide, picked, block)
    here = wide[pl.ds(pl.multiple_of(base, 128), block), :].astype(BF16)
    there = picked[...].astype(BF16)
    group = len(chunks) * 2 * half
    for j, k in enumerate(chunks):
        both = 2 if k == 0 else 1
        rows = outs[j].shape[0]
        row, lane = iota((rows, lanes), 0), iota((rows, lanes), 1)
        irrep, rest = row // (both * half), row % (both * half)
        side, rank = rest // half, rest % half
        start = irrep * group + j * 2 * half + rank
        mine = (lane == start + side * half).astype(F32).astype(BF16)
        other = (lane == start + (1 - side) * half).astype(F32).astype(BF16)
        outs[j][...] = (
            lax.dot_general(mine, here, NT, preferred_element_type=F32)
            + lax.dot_general(other, there, NT, preferred_element_type=F32)
        ).astype(BF16)


def block_of(slab):
    for tiles in (15, 10, 5, 3, 2, 1):
        block = tiles * 128
        if slab % block == 0:
            return block


def symmetrize(where, col_mirror, parts, chunks, owned, half):
    holders = len(parts)
    share, lanes = parts[0].shape
    slab = col_mirror.shape[0]
    block = block_of(slab)
    rows = [owned * half * (2 if k == 0 else 1) for k in chunks]
    return pl.pallas_call(
        functools.partial(symmetrize_kernel, holders, chunks, owned, half),
        grid_spec=pltpu.PrefetchScalarGridSpec(
            num_scalar_prefetch=2,
            grid=(slab // block,),
            in_specs=[pl.BlockSpec(memory_space=pl.ANY)] * holders,
            out_specs=[pl.BlockSpec((n, block), lambda s, w, m: (0, s)) for n in rows],
            scratch_shapes=[
                pltpu.VMEM((holders, share, lanes), BF16),
                pltpu.VMEM((slab, lanes), F32),
                pltpu.VMEM((block, lanes), F32),
                pltpu.SemaphoreType.DMA((holders,)),
            ],
        ),
        out_shape=[jax.ShapeDtypeStruct((n, slab), BF16) for n in rows],
        compiler_params=params(),
        cost_estimate=pl.CostEstimate(
            flops=4 * sum(rows) * lanes * slab + 40000 * slab, bytes_accessed=16 * slab * lanes, transcendentals=0
        ),
        name="symmetrize",
    )(where, col_mirror, *parts)


def finish_kernel(cols, owned, half, where_ref, mirror_ref, slot_ref, *refs):
    own_ref = refs[0]
    sums = refs[1:cols]
    out_ref, wide, picked = refs[cols:]
    step = pl.program_id(0)
    slab, lanes = wide.shape
    block = picked.shape[0]
    pairs = out_ref.shape[0]
    sent = owned * half
    used = (cols - 1) * sent

    @pl.when(step == 0)
    def _():
        def widen(n, carry):
            at = pl.ds(pl.multiple_of(n * block, 128), block)
            rows = [s[:, at].astype(F32) for s in sums]
            if lanes > used:
                rows.append(jnp.zeros((lanes - used, block), F32))
            wide[at, :] = jnp.concatenate(rows, axis=0).T
            return carry

        lax.fori_loop(0, slab // block, widen, 0)

    base = step * block
    gather_rows(mirror_ref, base, wide, picked, block)
    there = picked[...].astype(BF16)
    here = pl.ds(pl.multiple_of(base, 128), block)
    slot = jnp.broadcast_to(slot_ref[...], (pairs, pairs)).astype(F32).T.astype(I32)
    col = where_ref[1]
    own = own_ref.shape[0]
    slot_own = slot[:, :1]
    onehot = (slot_own == col * own + iota((pairs, own), 1)).astype(F32).astype(BF16)
    total = lax.dot_general(onehot, own_ref[...], NN, preferred_element_type=F32)
    for k in range(1, cols):
        at = iota((pairs, sent), 1)
        at = (col ^ k) * own + (at // half) * (2 * half) + at % half
        onehot = (slot_own == at).astype(F32).astype(BF16)
        total += lax.dot_general(onehot, sums[k - 1][:, here], NN, preferred_element_type=F32)
    at = iota((pairs, lanes), 1)
    rest = at % sent
    at = jnp.where(
        at < used, (col ^ (at // sent + 1)) * own + (rest // half) * (2 * half) + half + rest % half, -1
    )
    onehot = (slot_own == at).astype(F32).astype(BF16)
    total += lax.dot_general(onehot, there, NT, preferred_element_type=F32)
    out_ref[...] = total.astype(BF16)


def finish(where, col_mirror, slot, own, sums, owned, half):
    cols = len(sums) + 1
    slab = col_mirror.shape[0]
    pairs = slot.shape[1]
    block = block_of(slab)
    lanes = pl.cdiv(len(sums) * owned * half, 128) * 128
    return pl.pallas_call(
        functools.partial(finish_kernel, cols, owned, half),
        grid_spec=pltpu.PrefetchScalarGridSpec(
            num_scalar_prefetch=2,
            grid=(slab // block,),
            in_specs=[
                pl.BlockSpec((1, pairs), lambda s, w, m: (0, 0)),
                pl.BlockSpec((own.shape[0], block), lambda s, w, m: (0, s)),
            ]
            + [pl.BlockSpec((owned * half, slab), lambda s, w, m: (0, 0))] * len(sums),
            out_specs=pl.BlockSpec((pairs, block), lambda s, w, m: (0, s)),
            scratch_shapes=[pltpu.VMEM((slab, lanes), F32), pltpu.VMEM((block, lanes), F32)],
        ),
        out_shape=jax.ShapeDtypeStruct((pairs, slab), BF16),
        compiler_params=params(),
        cost_estimate=pl.CostEstimate(
            flops=2 * pairs * 256 * slab + 40000 * slab, bytes_accessed=8 * slab * lanes, transcendentals=0
        ),
        name="finish",
    )(where, col_mirror, slot, own, *sums)


def swap(array, axis, offset):
    return lax.ppermute(array, axis, [(i, i ^ offset) for i in range(lax.axis_size(axis))])


def gather_row_axis(chunk, order):
    held = {0: chunk}
    for bit in order:
        held.update({offset ^ bit: swap(array, "row", bit) for offset, array in list(held.items())})
    return held


def body(amplitudes, integrals, irreps, row_mirror, col_mirror):
    rows, cols = lax.axis_size("row"), lax.axis_size("col")
    owned = integrals.shape[0]
    pairs = amplitudes.shape[0]
    slots = pairs // 4
    half = slots // 2
    where = jnp.stack([lax.axis_index("row"), lax.axis_index("col")]).astype(I32)
    slot, packed = pack(where, irreps[None], row_mirror[None], amplitudes, cols, owned, half)
    chunks = [packed[0]] + [swap(packed[k], "col", k) for k in range(1, cols)]
    bits = [1 << b for b in range(rows.bit_length() - 1)]
    outer, core = bits[1:], bits[:1]
    size = max(1, 4 // owned)
    sums = {}
    for first in range(0, cols, size):
        batch = tuple(range(first, min(first + size, cols)))
        held = []
        for j, k in enumerate(batch):
            turn = j % len(outer)
            held.append(gather_row_axis(chunks[k], outer[turn:] + outer[:turn] + core))
        pieces = [held[j][o] for o in range(rows) for j in range(len(batch))]
        parts = product(pieces, integrals, rows, len(batch), slots)
        parts = [parts[0]] + [swap(parts[o], "row", o) for o in range(1, rows)]
        for k, part in zip(batch, symmetrize(where, col_mirror, parts, batch, owned, half)):
            sums[k] = part if k == 0 else swap(part, "col", k)
    return finish(where, col_mirror, slot, sums[0], [sums[k] for k in range(1, cols)], owned, half)


def solution(mesh):
    return jax.shard_map(
        body,
        mesh=mesh,
        in_specs=(
            P(("row", "col"), None),
            P("col", None, "row"),
            P(("row", "col")),
            P(("row", "col")),
            P(),
        ),
        out_specs=P(("row", "col"), None),
        check_vma=False,
    )
```

```python
import functools

import jax
import jax.numpy as jnp
from jax import lax
from jax.experimental import pallas as pl
from jax.experimental.pallas import tpu as pltpu
from jax.sharding import PartitionSpec as P

IRREPS = 8
F32, BF16, I32 = jnp.float32, jnp.bfloat16, jnp.int32
NN = (((1,), (0,)), ((), ()))
NT = (((1,), (1,)), ((), ()))
VMEM_LIMIT = 24 * 1024 * 1024
LADDER_LIMIT = 56 * 1024 * 1024


def iota(shape, dim):
    return lax.broadcasted_iota(I32, shape, dim)


def params(limit=VMEM_LIMIT):
    return pltpu.CompilerParams(vmem_limit_bytes=limit)


def pack_kernel(cols, owned, half, where_ref, irreps_ref, mirror_ref, amp_ref, slot_ref, *out_refs):
    pairs = irreps_ref.shape[1]
    square = (pairs, pairs)
    irreps = jnp.broadcast_to(irreps_ref[...], square)
    mirror = jnp.broadcast_to(mirror_ref[...], square)
    irreps_t = irreps.astype(F32).T.astype(I32)
    mirror_t = mirror.astype(F32).T.astype(I32)
    down, across = iota(square, 0), iota(square, 1)
    first = jnp.minimum(across, mirror)
    counted = (mirror_t > down) & (irreps_t == irreps) & (down < first)
    rank = jnp.sum(counted.astype(I32), axis=0, keepdims=True)
    partner = (across[:1] != first[:1]).astype(I32)
    slot = irreps_ref[...] * (2 * half) + partner * half + rank
    slot_ref[...] = slot
    rows = owned * 2 * half
    amp = amp_ref[...]
    for k in range(cols):
        base = (where_ref[1] ^ k) * rows
        onehot = (slot == base + iota((rows, pairs), 0)).astype(F32).astype(BF16)
        out_refs[k][...] = lax.dot_general(onehot, amp, NN, preferred_element_type=F32).astype(BF16)


def pack(where, irreps, mirror, amplitudes, cols, owned, half):
    pairs, contract = amplitudes.shape
    rows = owned * 2 * half
    whole = lambda shape: pl.BlockSpec(shape, lambda i, w: (0, 0))
    out = pl.pallas_call(
        functools.partial(pack_kernel, cols, owned, half),
        grid_spec=pltpu.PrefetchScalarGridSpec(
            num_scalar_prefetch=1,
            grid=(1,),
            in_specs=[whole((1, pairs)), whole((1, pairs)), whole((pairs, contract))],
            out_specs=[whole((1, pairs))] + [whole((rows, contract))] * cols,
        ),
        out_shape=[jax.ShapeDtypeStruct((1, pairs), I32)]
        + [jax.ShapeDtypeStruct((rows, contract), BF16)] * cols,
        compiler_params=params(),
        cost_estimate=pl.CostEstimate(
            flops=2 * cols * rows * pairs * contract, bytes_accessed=3 * pairs * contract * 2, transcendentals=0
        ),
        name="pack",
    )(where, irreps, mirror, amplitudes)
    return out[0], out[1:]


def product_kernel(holders, chunk_count, owned, slots, *refs):
    pieces = refs[: holders * chunk_count]
    integrals_ref = refs[holders * chunk_count]
    outs = refs[holders * chunk_count + 1 : holders * chunk_count + 1 + holders]
    rows_ref, sem = refs[-2:]
    group = chunk_count * slots

    @pl.when(pl.program_id(0) == 0)
    def _():
        copies = []
        for o in range(holders):
            for j in range(chunk_count):
                for i in range(owned):
                    n = len(copies)
                    copies.append(
                        pltpu.make_async_copy(
                            pieces[o * chunk_count + j].at[pl.ds(i * slots, slots)],
                            rows_ref.at[i, pl.ds(o * group + j * slots, slots)],
                            sem.at[n],
                        )
                    )
        for copy in copies:
            copy.start()
        for copy in copies:
            copy.wait()

    ladder = [
        lax.dot_general(integrals_ref[i], rows_ref[i], NT, preferred_element_type=F32) for i in range(owned)
    ]
    for o in range(holders):
        here = slice(o * group, (o + 1) * group)
        outs[o][...] = jnp.concatenate([ladder[i][:, here] for i in range(owned)], axis=1).astype(BF16)


def product(pieces, integrals, holders, chunk_count, slots):
    owned, share, contract = integrals.shape
    tile = 240
    group = chunk_count * slots
    lanes = owned * group
    return pl.pallas_call(
        functools.partial(product_kernel, holders, chunk_count, owned, slots),
        grid=(pl.cdiv(share, tile),),
        in_specs=[pl.BlockSpec(memory_space=pl.ANY)] * (holders * chunk_count)
        + [pl.BlockSpec((owned, tile, contract), lambda s: (0, s, 0))],
        out_specs=[pl.BlockSpec((tile, lanes), lambda s: (s, 0))] * holders,
        out_shape=[jax.ShapeDtypeStruct((share, lanes), BF16)] * holders,
        scratch_shapes=[
            pltpu.VMEM((owned, holders * group, contract), BF16),
            pltpu.SemaphoreType.DMA((holders * chunk_count * owned,)),
        ],
        compiler_params=params(LADDER_LIMIT),
        cost_estimate=pl.CostEstimate(
            flops=2 * owned * holders * group * contract * share,
            bytes_accessed=2 * owned * contract * (share + holders * group),
            transcendentals=0,
        ),
        name="ladder",
    )(*pieces, integrals)


def gather_rows(mirror_ref, base, source, target, count):
    step = 64

    def some(n, carry):
        at = n * step
        rows = [source[pl.ds(mirror_ref[base + at + u], 1), :] for u in range(step)]
        for u in range(step):
            target[pl.ds(at + u, 1), :] = rows[u]
        return carry

    lax.fori_loop(0, count // step, some, 0)


def symmetrize_kernel(holders, chunks, owned, half, where_ref, mirror_ref, *refs):
    parts = refs[:holders]
    outs = refs[holders : holders + len(chunks)]
    raw, wide, picked, sem = refs[holders + len(chunks) :]
    share = parts[0].shape[0]
    lanes = raw.shape[2]
    block = picked.shape[0]
    step = pl.program_id(0)

    @pl.when(step == 0)
    def _():
        copies = []
        for o in range(holders):
            copies.append(pltpu.make_async_copy(parts[o], raw.at[o], sem.at[o]))
        for copy in copies:
            copy.start()
        for o in range(holders):
            copies[o].wait()
            at = pl.multiple_of((where_ref[0] ^ o) * share, 8)
            wide[pl.ds(at, share), :] = raw[o].astype(F32)

    base = step * block
    gather_rows(mirror_ref, base, wide, picked, block)
    here = wide[pl.ds(pl.multiple_of(base, 128), block), :].astype(BF16)
    both = jnp.concatenate([here, picked[...].astype(BF16)], axis=1)
    group = len(chunks) * 2 * half
    picks = []
    for j, k in enumerate(chunks):
        sides = 2 if k == 0 else 1
        shape = (outs[j].shape[0], lanes)
        row, lane = iota(shape, 0), iota(shape, 1)
        irrep, rest = row // (sides * half), row % (sides * half)
        side, rank = rest // half, rest % half
        start = irrep * group + j * 2 * half + rank
        mine = lane == start + side * half
        other = lane == start + (1 - side) * half
        picks.append(jnp.concatenate([mine.astype(F32), other.astype(F32)], axis=1))
    pick = jnp.concatenate(picks, axis=0).astype(BF16)
    total = lax.dot_general(pick, both, NT, preferred_element_type=F32).astype(BF16)
    at = 0
    for out in outs:
        out[...] = total[at : at + out.shape[0]]
        at += out.shape[0]


def block_of(slab):
    for tiles in (15, 10, 5, 3, 2, 1):
        block = tiles * 128
        if slab % block == 0:
            return block


def symmetrize(where, col_mirror, parts, chunks, owned, half):
    holders = len(parts)
    share, lanes = parts[0].shape
    slab = col_mirror.shape[0]
    block = block_of(slab)
    rows = [owned * half * (2 if k == 0 else 1) for k in chunks]
    return pl.pallas_call(
        functools.partial(symmetrize_kernel, holders, chunks, owned, half),
        grid_spec=pltpu.PrefetchScalarGridSpec(
            num_scalar_prefetch=2,
            grid=(slab // block,),
            in_specs=[pl.BlockSpec(memory_space=pl.ANY)] * holders,
            out_specs=[pl.BlockSpec((n, block), lambda s, w, m: (0, s)) for n in rows],
            scratch_shapes=[
                pltpu.VMEM((holders, share, lanes), BF16),
                pltpu.VMEM((slab, lanes), F32),
                pltpu.VMEM((block, lanes), F32),
                pltpu.SemaphoreType.DMA((holders,)),
            ],
        ),
        out_shape=[jax.ShapeDtypeStruct((n, slab), BF16) for n in rows],
        compiler_params=params(),
        cost_estimate=pl.CostEstimate(
            flops=4 * sum(rows) * lanes * slab + 40000 * slab, bytes_accessed=16 * slab * lanes, transcendentals=0
        ),
        name="symmetrize",
    )(where, col_mirror, *parts)


def finish_kernel(cols, owned, half, where_ref, mirror_ref, slot_ref, *refs):
    own_ref = refs[0]
    sums = refs[1:cols]
    out_ref, wide, picked = refs[cols:]
    step = pl.program_id(0)
    slab, lanes = wide.shape
    block = picked.shape[0]
    pairs = out_ref.shape[0]
    sent = owned * half
    used = (cols - 1) * sent

    @pl.when(step == 0)
    def _():
        def widen(n, carry):
            at = pl.ds(pl.multiple_of(n * block, 128), block)
            rows = [s[:, at].astype(F32) for s in sums]
            if lanes > used:
                rows.append(jnp.zeros((lanes - used, block), F32))
            wide[at, :] = jnp.concatenate(rows, axis=0).T
            return carry

        lax.fori_loop(0, slab // block, widen, 0)

    base = step * block
    gather_rows(mirror_ref, base, wide, picked, block)
    there = picked[...].astype(BF16)
    here = pl.ds(pl.multiple_of(base, 128), block)
    slot = jnp.broadcast_to(slot_ref[...], (pairs, pairs)).astype(F32).T.astype(I32)
    col = where_ref[1]
    own = own_ref.shape[0]
    slot_own = slot[:, :1]
    onehot = (slot_own == col * own + iota((pairs, own), 1)).astype(F32).astype(BF16)
    total = lax.dot_general(onehot, own_ref[...], NN, preferred_element_type=F32)
    for k in range(1, cols):
        at = iota((pairs, sent), 1)
        at = (col ^ k) * own + (at // half) * (2 * half) + at % half
        onehot = (slot_own == at).astype(F32).astype(BF16)
        total += lax.dot_general(onehot, sums[k - 1][:, here], NN, preferred_element_type=F32)
    at = iota((pairs, lanes), 1)
    rest = at % sent
    at = jnp.where(
        at < used, (col ^ (at // sent + 1)) * own + (rest // half) * (2 * half) + half + rest % half, -1
    )
    onehot = (slot_own == at).astype(F32).astype(BF16)
    total += lax.dot_general(onehot, there, NT, preferred_element_type=F32)
    out_ref[...] = total.astype(BF16)


def finish(where, col_mirror, slot, own, sums, owned, half):
    cols = len(sums) + 1
    slab = col_mirror.shape[0]
    pairs = slot.shape[1]
    block = block_of(slab)
    lanes = pl.cdiv(len(sums) * owned * half, 128) * 128
    return pl.pallas_call(
        functools.partial(finish_kernel, cols, owned, half),
        grid_spec=pltpu.PrefetchScalarGridSpec(
            num_scalar_prefetch=2,
            grid=(slab // block,),
            in_specs=[
                pl.BlockSpec((1, pairs), lambda s, w, m: (0, 0)),
                pl.BlockSpec((own.shape[0], block), lambda s, w, m: (0, s)),
            ]
            + [pl.BlockSpec((owned * half, slab), lambda s, w, m: (0, 0))] * len(sums),
            out_specs=pl.BlockSpec((pairs, block), lambda s, w, m: (0, s)),
            scratch_shapes=[pltpu.VMEM((slab, lanes), F32), pltpu.VMEM((block, lanes), F32)],
        ),
        out_shape=jax.ShapeDtypeStruct((pairs, slab), BF16),
        compiler_params=params(),
        cost_estimate=pl.CostEstimate(
            flops=2 * pairs * 256 * slab + 40000 * slab, bytes_accessed=8 * slab * lanes, transcendentals=0
        ),
        name="finish",
    )(where, col_mirror, slot, own, *sums)


def swap(array, axis, offset):
    return lax.ppermute(array, axis, [(i, i ^ offset) for i in range(lax.axis_size(axis))])


def after(arrays, earlier):
    earlier = tuple(earlier)
    return list(lax.optimization_barrier((tuple(arrays), earlier))[0]) if earlier else list(arrays)


def spread(chunk, order):
    return {0: chunk, **{bit: swap(chunk, "row", bit) for bit in order}}


def forward(held, order):
    reach = [0]
    fresh = []
    for bit in order:
        for offset in list(reach):
            if offset ^ bit not in held:
                held[offset ^ bit] = swap(held[offset], "row", bit)
                fresh.append(offset ^ bit)
            reach.append(offset ^ bit)
    return fresh


def share_cores(held, core, offsets):
    for bit in core:
        for offset in list(offsets):
            held[offset ^ bit] = swap(held[offset], "row", bit)
    return [held[offset ^ bit] for bit in core for offset in offsets]


def gate(held, earlier):
    offsets = list(held)
    held.update(zip(offsets, after([held[o] for o in offsets], earlier)))


def body(amplitudes, integrals, irreps, row_mirror, col_mirror):
    rows, cols = lax.axis_size("row"), lax.axis_size("col")
    owned = integrals.shape[0]
    pairs = amplitudes.shape[0]
    slots = pairs // 4
    half = slots // 2
    where = jnp.stack([lax.axis_index("row"), lax.axis_index("col")]).astype(I32)
    slot, packed = pack(where, irreps[None], row_mirror[None], amplitudes, cols, owned, half)
    bits = [1 << b for b in range(rows.bit_length() - 1)]
    outer, core = bits[1:], bits[:1]
    turns = max(1, cols // max(1, 4 // owned))
    batches = [tuple(range(first, cols, turns)) for first in range(turns)]
    integrals_t = jnp.swapaxes(integrals, 1, 2)

    ready = {}
    for k in range(cols):
        early = () if k < 3 else (ready[k - 1],)
        ready[k] = swap(after([packed[k]], early)[0], "col", k) if k else packed[0]

    combined = range(2, rows, 2)
    held, parts = {}, []
    turned = []
    for n, batch in enumerate(batches):
        if n == 0:
            for j, k in enumerate(batch):
                chunk = ready[k]
                if j:
                    (chunk,) = after([chunk], [ready[k - 1], *turned])
                held[k] = {0: chunk, **{o: swap(chunk, "row", o) for o in combined}}
                turned = [held[k][o] for o in combined]
                last = combined[-1]
                share_cores(held[k], core, [o for o in held[k] if o != last])
                if j and k + 1 < cols:
                    (held[k][last],) = after([held[k][last]], [ready[k + 1]])
                share_cores(held[k], core, [last])
        else:
            turned = []
            for j, k in enumerate(batch):
                turn = j % len(outer)
                order = outer[turn:] + outer[:turn]
                held[k] = spread(ready[k], order)
            for j, k in enumerate(batch):
                turn = j % len(outer)
                order = outer[turn:] + outer[:turn]
                gate(held[k], parts[-1][1:2])
                first = list(held[k])
                fresh = forward(held[k], order)
                turned += [held[k][o] for o in fresh]
                share_cores(held[k], core, first)
                share_cores(held[k], core, fresh)
        pieces = [held[k][o] for o in range(rows) for k in batch]
        parts.append(product(pieces, integrals_t, rows, len(batch), slots))

    far = sorted(range(1, rows), key=lambda o: (-(o >> 1).bit_count(), -o))
    sums = {}
    hidden = [part[:1] for part in parts[1:]]
    last = turned
    for n, (batch, part) in enumerate(zip(batches, parts)):
        part = list(part)
        for m, o in enumerate(far):
            earlier = list(last) if n or m >= 2 else []
            if m >= len(far) - 2 and n < len(hidden) + 1:
                earlier += [part[f] for f in far[:2]] + list(hidden[n] if n < len(hidden) else totals[:1])
            part[o] = swap(after([part[o]], earlier)[0], "row", o)
        last = [part[o] for o in far]
        totals = symmetrize(where, col_mirror, part, batch, owned, half)
        for k, total in zip(batch, totals):
            sums[k] = total if k == 0 else swap(total, "col", k)
    return finish(where, col_mirror, slot, sums[0], [sums[k] for k in range(1, cols)], owned, half)


def solution(mesh):
    return jax.shard_map(
        body,
        mesh=mesh,
        in_specs=(
            P(("row", "col"), None),
            P("col", None, "row"),
            P(("row", "col")),
            P(("row", "col")),
            P(),
        ),
        out_specs=P(("row", "col"), None),
        check_vma=False,
    )
```

```python
import functools

import jax
import jax.numpy as jnp
from jax import lax
from jax.experimental import pallas as pl
from jax.experimental.pallas import tpu as pltpu
from jax.sharding import PartitionSpec as P

IRREPS = 8
F32, BF16, I32 = jnp.float32, jnp.bfloat16, jnp.int32
NN = (((1,), (0,)), ((), ()))
NT = (((1,), (1,)), ((), ()))
VMEM_LIMIT = 24 * 1024 * 1024
LADDER_LIMIT = 56 * 1024 * 1024
TILE = 128


def iota(shape, dim):
    return lax.broadcasted_iota(I32, shape, dim)


def params(limit=VMEM_LIMIT):
    return pltpu.CompilerParams(vmem_limit_bytes=limit)


def pack_kernel(cols, owned, half, where_ref, irreps_ref, mirror_ref, amp_ref, slot_ref, *out_refs):
    pairs = irreps_ref.shape[1]
    square = (pairs, pairs)
    irreps = jnp.broadcast_to(irreps_ref[...], square)
    mirror = jnp.broadcast_to(mirror_ref[...], square)
    irreps_t = irreps.astype(F32).T.astype(I32)
    mirror_t = mirror.astype(F32).T.astype(I32)
    down, across = iota(square, 0), iota(square, 1)
    first = jnp.minimum(across, mirror)
    counted = (mirror_t > down) & (irreps_t == irreps) & (down < first)
    rank = jnp.sum(counted.astype(I32), axis=0, keepdims=True)
    partner = (across[:1] != first[:1]).astype(I32)
    slot = irreps_ref[...] * (2 * half) + partner * half + rank
    slot_ref[...] = slot
    rows = owned * 2 * half
    amp = amp_ref[...]
    for k in range(cols):
        base = (where_ref[1] ^ k) * rows
        onehot = (slot == base + iota((rows, pairs), 0)).astype(F32).astype(BF16)
        out_refs[k][...] = lax.dot_general(onehot, amp, NN, preferred_element_type=F32).astype(BF16)


def pack(where, irreps, mirror, amplitudes, cols, owned, half):
    pairs, contract = amplitudes.shape
    rows = owned * 2 * half
    whole = lambda shape: pl.BlockSpec(shape, lambda i, w: (0, 0))
    out = pl.pallas_call(
        functools.partial(pack_kernel, cols, owned, half),
        grid_spec=pltpu.PrefetchScalarGridSpec(
            num_scalar_prefetch=1,
            grid=(1,),
            in_specs=[whole((1, pairs)), whole((1, pairs)), whole((pairs, contract))],
            out_specs=[whole((1, pairs))] + [whole((rows, contract))] * cols,
        ),
        out_shape=[jax.ShapeDtypeStruct((1, pairs), I32)]
        + [jax.ShapeDtypeStruct((rows, contract), BF16)] * cols,
        compiler_params=params(),
        cost_estimate=pl.CostEstimate(
            flops=2 * cols * rows * pairs * contract, bytes_accessed=3 * pairs * contract * 2, transcendentals=0
        ),
        name="pack",
    )(where, irreps, mirror, amplitudes)
    return out[0], out[1:]


def product_kernel(holders, chunk_count, owned, slots, places, array_count, *refs):
    arrays = refs[:array_count]
    integrals_ref, rows_ref, sem = refs[array_count], *refs[-2:]
    outs = refs[array_count + 1 : -2]
    group = chunk_count * slots

    @pl.when(pl.program_id(0) == 0)
    def _():
        copies = []
        for i in range(owned):
            for (o, j), (at, row) in places.items():
                n = len(copies)
                copies.append(
                    pltpu.make_async_copy(
                        arrays[at].at[pl.ds(row + i * slots, slots)],
                        rows_ref.at[i, pl.ds(o * group + j * slots, slots)],
                        sem.at[n],
                    )
                )
        for copy in copies:
            copy.start()
        for copy in copies:
            copy.wait()

    ladder = [
        lax.dot_general(integrals_ref[i], rows_ref[i], NT, preferred_element_type=F32) for i in range(owned)
    ]
    for o in range(holders):
        here = slice(o * group, (o + 1) * group)
        block = jnp.concatenate([ladder[i][:, here] for i in range(owned)], axis=1).astype(BF16)
        if len(outs) == 2:
            outs[o % 2][o // 2] = block
        else:
            outs[o][...] = block


def product(arrays, places, integrals, holders, chunk_count, slots, joined):
    owned, share, contract = integrals.shape
    tile = 240
    group = chunk_count * slots
    lanes = owned * group
    if joined:
        spec = pl.BlockSpec((holders // 2, tile, lanes), lambda s: (0, s, 0))
        out = jax.ShapeDtypeStruct((holders // 2, share, lanes), BF16)
    else:
        spec = pl.BlockSpec((tile, lanes), lambda s: (s, 0))
        out = jax.ShapeDtypeStruct((share, lanes), BF16)
    return pl.pallas_call(
        functools.partial(product_kernel, holders, chunk_count, owned, slots, places, len(arrays)),
        grid=(pl.cdiv(share, tile),),
        in_specs=[pl.BlockSpec(memory_space=pl.ANY)] * len(arrays)
        + [pl.BlockSpec((owned, tile, contract), lambda s: (0, s, 0))],
        out_specs=[spec] * (2 if joined else holders),
        out_shape=[out] * (2 if joined else holders),
        scratch_shapes=[
            pltpu.VMEM((owned, holders * group, contract), BF16),
            pltpu.SemaphoreType.DMA((holders * chunk_count * owned,)),
        ],
        compiler_params=params(LADDER_LIMIT),
        cost_estimate=pl.CostEstimate(
            flops=2 * owned * holders * group * contract * share,
            bytes_accessed=2 * owned * contract * (share + holders * group),
            transcendentals=0,
        ),
        name="ladder",
    )(*arrays, integrals)


def gather_rows(mirror_ref, base, source, target):
    rows = [source[pl.ds(mirror_ref[base + u], 1), :] for u in range(target.shape[0])]
    for u, row in enumerate(rows):
        target[u : u + 1, :] = row


def runs_of(slab):
    tiles = slab // TILE
    return next(n for n in (15, 5, 3, 4, 2, 1) if tiles % n == 0), 1


def symmetrize_kernel(places, array_count, chunks, owned, half, run, turns, where_ref, mirror_ref, *refs):
    holders = len(places)
    parts, refs = refs[:array_count], refs[array_count:]
    outs, refs = refs[: len(chunks)], refs[len(chunks) :]
    raw, wide, sem, *picked = refs
    share, lanes = raw.shape[1:]
    step = pl.program_id(0)

    @pl.when(step == 0)
    def _():
        copies = []
        for o in range(holders):
            at, index = places[o]
            part = parts[at] if index is None else parts[at].at[index]
            copies.append(pltpu.make_async_copy(part, raw.at[o], sem.at[o]))
        for copy in copies:
            copy.start()
        for o in range(holders):
            copies[o].wait()
            at = pl.multiple_of((where_ref[0] ^ o) * share, 8)
            wide[pl.ds(at, share), :] = raw[o].astype(F32)

    group = len(chunks) * 2 * half
    picks = []
    for j, k in enumerate(chunks):
        sides = 2 if k == 0 else 1
        shape = (outs[j].shape[0], lanes)
        row, lane = iota(shape, 0), iota(shape, 1)
        irrep, rest = row // (sides * half), row % (sides * half)
        side, rank = rest // half, rest % half
        start = irrep * group + j * 2 * half + rank
        mine = lane == start + side * half
        other = lane == start + (1 - side) * half
        picks.append(jnp.concatenate([mine.astype(F32), other.astype(F32)], axis=1))
    pick = jnp.concatenate(picks, axis=0).astype(BF16)

    def some(n, carry):
        for i in range(run):
            inside = pl.multiple_of((n * run + i) * TILE, TILE)
            base = step * (turns * run * TILE) + inside
            gather_rows(mirror_ref, base, wide, picked[i])
            here = wide[pl.ds(pl.multiple_of(base, TILE), TILE), :]
            both = jnp.concatenate([here, picked[i][...]], axis=1).astype(BF16)
            total = lax.dot_general(pick, both, NT, preferred_element_type=F32).astype(BF16)
            at = 0
            for out in outs:
                out[:, pl.ds(inside, TILE)] = total[at : at + out.shape[0]]
                at += out.shape[0]
        return carry

    lax.fori_loop(0, turns, some, 0)


def symmetrize(where, col_mirror, parts, places, chunks, owned, half):
    holders = len(places)
    share, lanes = parts[0].shape[-2:]
    slab = col_mirror.shape[0]
    run, turns = runs_of(slab)
    block = run * turns * TILE
    rows = [owned * half * (2 if k == 0 else 1) for k in chunks]
    return pl.pallas_call(
        functools.partial(symmetrize_kernel, places, len(parts), chunks, owned, half, run, turns),
        grid_spec=pltpu.PrefetchScalarGridSpec(
            num_scalar_prefetch=2,
            grid=(slab // block,),
            in_specs=[pl.BlockSpec(memory_space=pl.ANY)] * len(parts),
            out_specs=[pl.BlockSpec((n, block), lambda s, w, m: (0, s)) for n in rows],
            scratch_shapes=[
                pltpu.VMEM((holders, share, lanes), BF16),
                pltpu.VMEM((slab, lanes), F32),
                pltpu.SemaphoreType.DMA((holders,)),
            ]
            + [pltpu.VMEM((TILE, lanes), F32)] * run,
        ),
        out_shape=[jax.ShapeDtypeStruct((n, slab), BF16) for n in rows],
        compiler_params=params(),
        cost_estimate=pl.CostEstimate(
            flops=4 * sum(rows) * lanes * slab + 40000 * slab, bytes_accessed=16 * slab * lanes, transcendentals=0
        ),
        name="symmetrize",
    )(where, col_mirror, *parts)


def finish_kernel(cols, owned, half, run, turns, where_ref, mirror_ref, slot_ref, *refs):
    own_ref = refs[0]
    sums = refs[1:cols]
    out_ref, wide = refs[cols : cols + 2]
    picked = refs[cols + 2 :]
    step = pl.program_id(0)
    slab, lanes = wide.shape
    pairs = out_ref.shape[0]
    sent = owned * half
    used = (cols - 1) * sent
    block = run * turns * TILE

    @pl.when(step == 0)
    def _():
        def widen(n, carry):
            for i in range(run):
                at = pl.ds(pl.multiple_of((n * run + i) * TILE, TILE), TILE)
                rows = [s[:, at].astype(F32) for s in sums]
                if lanes > used:
                    rows.append(jnp.zeros((lanes - used, TILE), F32))
                wide[at, :] = jnp.concatenate(rows, axis=0).T
            return carry

        lax.fori_loop(0, slab // TILE // run, widen, 0)

    slot = jnp.broadcast_to(slot_ref[...], (pairs, pairs)).astype(F32).T.astype(I32)[:, :1]
    col = where_ref[1]
    own = own_ref.shape[0]
    onehots = [slot == col * own + iota((pairs, own), 1)]
    at = iota((pairs, used), 1)
    rest = at % sent
    first = (col ^ (at // sent + 1)) * own + (rest // half) * (2 * half) + rest % half
    onehots.append(slot == first)
    straight = jnp.concatenate([h.astype(F32) for h in onehots], axis=1).astype(BF16)
    second = [(slot == first + half).astype(F32)]
    if lanes > used:
        second.append(jnp.zeros((pairs, lanes - used), F32))
    crossed = jnp.concatenate(second, axis=1).astype(BF16)

    def some(n, carry):
        for i in range(run):
            inside = pl.multiple_of((n * run + i) * TILE, TILE)
            base = pl.multiple_of(step * block + inside, TILE)
            gather_rows(mirror_ref, base, wide, picked[i])
            rows = [own_ref[:, pl.ds(inside, TILE)]] + [s[:, pl.ds(base, TILE)] for s in sums]
            total = lax.dot_general(straight, jnp.concatenate(rows, axis=0), NN, preferred_element_type=F32)
            total += lax.dot_general(crossed, picked[i][...].astype(BF16), NT, preferred_element_type=F32)
            out_ref[:, pl.ds(inside, TILE)] = total.astype(BF16)
        return carry

    lax.fori_loop(0, turns, some, 0)


def finish(where, col_mirror, slot, own, sums, owned, half):
    cols = len(sums) + 1
    slab = col_mirror.shape[0]
    pairs = slot.shape[1]
    run, turns = runs_of(slab)
    block = run * turns * TILE
    lanes = pl.cdiv(len(sums) * owned * half, 128) * 128
    return pl.pallas_call(
        functools.partial(finish_kernel, cols, owned, half, run, turns),
        grid_spec=pltpu.PrefetchScalarGridSpec(
            num_scalar_prefetch=2,
            grid=(slab // block,),
            in_specs=[
                pl.BlockSpec((1, pairs), lambda s, w, m: (0, 0)),
                pl.BlockSpec((own.shape[0], block), lambda s, w, m: (0, s)),
            ]
            + [pl.BlockSpec((owned * half, slab), lambda s, w, m: (0, 0))] * len(sums),
            out_specs=pl.BlockSpec((pairs, block), lambda s, w, m: (0, s)),
            scratch_shapes=[pltpu.VMEM((slab, lanes), F32)] + [pltpu.VMEM((TILE, lanes), F32)] * run,
        ),
        out_shape=jax.ShapeDtypeStruct((pairs, slab), BF16),
        compiler_params=params(),
        cost_estimate=pl.CostEstimate(
            flops=2 * pairs * 256 * slab + 40000 * slab, bytes_accessed=8 * slab * lanes, transcendentals=0
        ),
        name="finish",
    )(where, col_mirror, slot, own, *sums)


def swap(array, axis, offset):
    return lax.ppermute(array, axis, [(i, i ^ offset) for i in range(lax.axis_size(axis))])


def after(arrays, earlier):
    earlier = tuple(earlier)
    return list(lax.optimization_barrier((tuple(arrays), earlier))[0]) if earlier else list(arrays)


def forward(held, order):
    reach = [0]
    fresh = []
    for bit in order:
        for offset in list(reach):
            if offset ^ bit not in held:
                held[offset ^ bit] = swap(held[offset], "row", bit)
                fresh.append(offset ^ bit)
            reach.append(offset ^ bit)
    return fresh


class Rows:
    def __init__(self):
        self.arrays, self.places = [], {}

    def add(self, keys, pieces):
        joined = jnp.concatenate(pieces) if len(pieces) > 1 else pieces[0]
        size = pieces[0].shape[0]
        for core, array in enumerate((joined, swap(joined, "row", 1))):
            for n, (offset, j) in enumerate(keys):
                self.places[offset ^ core, j] = (len(self.arrays), n * size)
            self.arrays.append(array)
        return self.arrays[-1]


def body(amplitudes, integrals, irreps, row_mirror, col_mirror):
    rows, cols = lax.axis_size("row"), lax.axis_size("col")
    owned = integrals.shape[0]
    pairs = amplitudes.shape[0]
    slots = pairs // 4
    half = slots // 2
    where = jnp.stack([lax.axis_index("row"), lax.axis_index("col")]).astype(I32)
    slot, packed = pack(where, irreps[None], row_mirror[None], amplitudes, cols, owned, half)
    outer = [1 << b for b in range(1, rows.bit_length() - 1)]
    combined = range(2, rows, 2)
    turns = max(1, cols // max(1, 4 // owned))
    batches = [tuple(range(first, cols, turns)) for first in range(turns)]
    integrals_t = jnp.swapaxes(integrals, 1, 2)

    ready = {}
    for k in range(cols):
        early = () if k < 3 else (ready[k - 1],)
        ready[k] = swap(after([packed[k]], early)[0], "col", k) if k else packed[0]

    parts = []
    for n, batch in enumerate(batches):
        gathered = Rows()
        held = []
        if n == 0:
            inner = []
            for j, k in enumerate(batch):
                (chunk,) = after([ready[k]], [ready[k - 1], *inner[:1]] if j else [])
                held = {0: chunk, **{o: swap(chunk, "row", o) for o in combined}}
                inner = [held[o] for o in combined[::-1]]
                if j == 0:
                    gathered.add([(o, j) for o in held], list(held.values()))
                    continue
                near, far = outer, [o for o in held if o not in outer]
                gathered.add([(o, j) for o in near], [held[o] for o in near])
                early = [ready[k + 1]] if k + 1 < cols else []
                gathered.add([(o, j) for o in far], after([held[o] for o in far], early))
        else:
            keys, pieces, fresh = [], [], []
            for j, k in enumerate(batch):
                held.append({0: ready[k], **{bit: swap(ready[k], "row", bit) for bit in outer}})
            for j, k in enumerate(batch):
                offsets = list(held[j])
                held[j] = dict(zip(offsets, after([held[j][o] for o in offsets], parts[-1][:1])))
                turn = j % len(outer)
                keys += [(o, j) for o in offsets]
                fresh += [(o, j) for o in forward(held[j], outer[turn:] + outer[:turn])]
            gathered.add(keys, [held[j][o] for o, j in keys])
            gathered.add(fresh, [held[j][o] for o, j in fresh])
        arrays = after(gathered.arrays, [part[1] for part in parts[-1:]])
        joined = n + 1 < turns
        part = list(product(arrays, gathered.places, integrals_t, rows, len(batch), slots, joined))
        if joined:
            part[1] = swap(part[1], "row", 1)
        parts.append(part)

    sums = {}
    totals, last = (), ()
    for n, (batch, part) in enumerate(zip(batches, parts)):
        if n + 1 < turns:
            pieces = list(part)
            for o in combined:
                both = jnp.concatenate([array[o // 2 : o // 2 + 1] for array in part])
                pieces.append(swap(both, "row", o))
            last = pieces[2:]
            places = [(o, 0) if o < 2 else (o // 2 + 1, o % 2) for o in range(rows)]
        else:
            far = sorted(range(1, rows), key=lambda o: (-(o >> 1).bit_count(), -o))
            pieces = list(part)
            for m, o in enumerate(far):
                early = [*totals, *(pieces[f] for f in far[:2])] if m >= len(far) - 2 else last
                pieces[o] = swap(after([pieces[o]], early)[0], "row", o)
            places = [(o, None) for o in range(rows)]
        totals = symmetrize(where, col_mirror, pieces, places, batch, owned, half)
        for k, total in zip(batch, totals):
            sums[k] = total if k == 0 else swap(total, "col", k)
        totals = totals[:1]
    return finish(where, col_mirror, slot, sums[0], [sums[k] for k in range(1, cols)], owned, half)


def solution(mesh):
    return jax.shard_map(
        body,
        mesh=mesh,
        in_specs=(
            P(("row", "col"), None),
            P("col", None, "row"),
            P(("row", "col")),
            P(("row", "col")),
            P(),
        ),
        out_specs=P(("row", "col"), None),
        check_vma=False,
    )
```

```python
import functools
import math

import jax
import jax.numpy as jnp
from jax import lax
from jax.experimental import pallas as pl
from jax.experimental.pallas import tpu as pltpu
from jax.sharding import PartitionSpec as P

IRREPS = 8
F32, BF16, I32 = jnp.float32, jnp.bfloat16, jnp.int32
NN = (((1,), (0,)), ((), ()))
NT = (((1,), (1,)), ((), ()))
VMEM_LIMIT = 24 * 1024 * 1024
LADDER_LIMIT = 56 * 1024 * 1024
TILE = 128


def iota(shape, dim):
    return lax.broadcasted_iota(I32, shape, dim)


def params(limit=VMEM_LIMIT):
    return pltpu.CompilerParams(vmem_limit_bytes=limit)


def pack_kernel(cols, owned, half, where_ref, irreps_ref, mirror_ref, amp_ref, slot_ref, *out_refs):
    pairs = irreps_ref.shape[1]
    square = (pairs, pairs)
    irreps = jnp.broadcast_to(irreps_ref[...], square)
    mirror = jnp.broadcast_to(mirror_ref[...], square)
    irreps_t = irreps.astype(F32).T.astype(I32)
    mirror_t = mirror.astype(F32).T.astype(I32)
    down, across = iota(square, 0), iota(square, 1)
    first = jnp.minimum(across, mirror)
    counted = (mirror_t > down) & (irreps_t == irreps) & (down < first)
    rank = jnp.sum(counted.astype(I32), axis=0, keepdims=True)
    partner = (across[:1] != first[:1]).astype(I32)
    slot = irreps_ref[...] * (2 * half) + partner * half + rank
    slot_ref[...] = slot
    rows = owned * 2 * half
    amp = amp_ref[...]
    for k in range(cols):
        base = (where_ref[1] ^ k) * rows
        onehot = (slot == base + iota((rows, pairs), 0)).astype(F32).astype(BF16)
        out_refs[k][...] = lax.dot_general(onehot, amp, NN, preferred_element_type=F32).astype(BF16)


def pack(where, irreps, mirror, amplitudes, cols, owned, half):
    pairs, contract = amplitudes.shape
    rows = owned * 2 * half
    whole = lambda shape: pl.BlockSpec(shape, lambda i, w: (0, 0))
    out = pl.pallas_call(
        functools.partial(pack_kernel, cols, owned, half),
        grid_spec=pltpu.PrefetchScalarGridSpec(
            num_scalar_prefetch=1,
            grid=(1,),
            in_specs=[whole((1, pairs)), whole((1, pairs)), whole((pairs, contract))],
            out_specs=[whole((1, pairs))] + [whole((rows, contract))] * cols,
        ),
        out_shape=[jax.ShapeDtypeStruct((1, pairs), I32)]
        + [jax.ShapeDtypeStruct((rows, contract), BF16)] * cols,
        compiler_params=params(),
        cost_estimate=pl.CostEstimate(
            flops=2 * cols * rows * pairs * contract, bytes_accessed=3 * pairs * contract * 2, transcendentals=0
        ),
        name="pack",
    )(where, irreps, mirror, amplitudes)
    return out[0], out[1:]


def product_kernel(holders, chunk_count, owned, slots, places, array_count, *refs):
    arrays = refs[:array_count]
    integrals_ref, rows_ref, sem = refs[array_count], *refs[-2:]
    outs = refs[array_count + 1 : -2]
    group = chunk_count * slots

    @pl.when(pl.program_id(0) == 0)
    def _():
        copies = []
        for i in range(owned):
            for (o, j), (at, row) in places.items():
                n = len(copies)
                copies.append(
                    pltpu.make_async_copy(
                        arrays[at].at[pl.ds(row + i * slots, slots)],
                        rows_ref.at[i, pl.ds(o * group + j * slots, slots)],
                        sem.at[n],
                    )
                )
        for copy in copies:
            copy.start()
        for copy in copies:
            copy.wait()

    ladder = [
        lax.dot_general(integrals_ref[i], rows_ref[i], NT, preferred_element_type=F32) for i in range(owned)
    ]
    for o in range(holders):
        here = slice(o * group, (o + 1) * group)
        block = jnp.concatenate([ladder[i][:, here] for i in range(owned)], axis=1).astype(BF16)
        if len(outs) == 2:
            outs[o % 2][o // 2] = block
        else:
            outs[o][...] = block


def product(arrays, places, integrals, holders, chunk_count, slots, joined):
    owned, share, contract = integrals.shape
    tile = 240
    group = chunk_count * slots
    lanes = owned * group
    if joined:
        spec = pl.BlockSpec((holders // 2, tile, lanes), lambda s: (0, s, 0))
        out = jax.ShapeDtypeStruct((holders // 2, share, lanes), BF16)
    else:
        spec = pl.BlockSpec((tile, lanes), lambda s: (s, 0))
        out = jax.ShapeDtypeStruct((share, lanes), BF16)
    return pl.pallas_call(
        functools.partial(product_kernel, holders, chunk_count, owned, slots, places, len(arrays)),
        grid=(pl.cdiv(share, tile),),
        in_specs=[pl.BlockSpec(memory_space=pl.ANY)] * len(arrays)
        + [pl.BlockSpec((owned, tile, contract), lambda s: (0, s, 0))],
        out_specs=[spec] * (2 if joined else holders),
        out_shape=[out] * (2 if joined else holders),
        scratch_shapes=[
            pltpu.VMEM((owned, holders * group, contract), BF16),
            pltpu.SemaphoreType.DMA((holders * chunk_count * owned,)),
        ],
        compiler_params=params(LADDER_LIMIT),
        cost_estimate=pl.CostEstimate(
            flops=2 * owned * holders * group * contract * share,
            bytes_accessed=2 * owned * contract * (share + holders * group),
            transcendentals=0,
        ),
        name="ladder",
    )(*arrays, integrals)


def gather_rows(mirror_ref, base, source, target):
    rows = [source[pl.ds(mirror_ref[base + u], 1), :] for u in range(target.shape[0])]
    for u, row in enumerate(rows):
        target[u : u + 1, :] = row


def runs_of(slab):
    tiles = slab // TILE
    return next(n for n in (15, 5, 3, 4, 2, 1) if tiles % n == 0), 1


def symmetrize_kernel(places, array_count, chunks, owned, half, run, turns, offset, where_ref, mirror_ref, *refs):
    holders = len(places)
    parts, refs = refs[:array_count], refs[array_count:]
    outs, refs = refs[: len(chunks)], refs[len(chunks) :]
    raw, wide, sem, *picked = refs
    share, lanes = raw.shape[1:]
    step = pl.program_id(0)

    @pl.when(step == 0)
    def _():
        copies = []
        for o in range(holders):
            at, index = places[o]
            part = parts[at] if index is None else parts[at].at[index]
            copies.append(pltpu.make_async_copy(part, raw.at[o], sem.at[o]))
        for copy in copies:
            copy.start()
        for o in range(holders):
            copies[o].wait()
            at = pl.multiple_of((where_ref[0] ^ o) * share, 8)
            wide[pl.ds(at, share), :] = raw[o].astype(F32)

    group = len(chunks) * 2 * half
    picks = []
    for j, k in enumerate(chunks):
        sides = 2 if k == 0 else 1
        shape = (outs[j].shape[0], lanes)
        row, lane = iota(shape, 0), iota(shape, 1)
        irrep, rest = row // (sides * half), row % (sides * half)
        side, rank = rest // half, rest % half
        start = irrep * group + j * 2 * half + rank
        mine = lane == start + side * half
        other = lane == start + (1 - side) * half
        picks.append(jnp.concatenate([mine.astype(F32), other.astype(F32)], axis=1))
    pick = jnp.concatenate(picks, axis=0).astype(BF16)

    def some(n, carry):
        for i in range(run):
            inside = pl.multiple_of((n * run + i) * TILE, TILE)
            base = (step + offset) * (turns * run * TILE) + inside
            gather_rows(mirror_ref, base, wide, picked[i])
            here = wide[pl.ds(pl.multiple_of(base, TILE), TILE), :]
            both = jnp.concatenate([here, picked[i][...]], axis=1).astype(BF16)
            total = lax.dot_general(pick, both, NT, preferred_element_type=F32).astype(BF16)
            at = 0
            for out in outs:
                out[:, pl.ds(inside, TILE)] = total[at : at + out.shape[0]]
                at += out.shape[0]
        return carry

    lax.fori_loop(0, turns, some, 0)


def symmetrize(where, col_mirror, parts, places, chunks, owned, half, first, blocks):
    holders = len(places)
    share, lanes = parts[0].shape[-2:]
    slab = col_mirror.shape[0]
    run, turns = runs_of(slab)
    block = run * turns * TILE
    rows = [owned * half * (2 if k == 0 else 1) for k in chunks]
    return pl.pallas_call(
        functools.partial(symmetrize_kernel, places, len(parts), chunks, owned, half, run, turns, first),
        grid_spec=pltpu.PrefetchScalarGridSpec(
            num_scalar_prefetch=2,
            grid=(blocks,),
            in_specs=[pl.BlockSpec(memory_space=pl.ANY)] * len(parts),
            out_specs=[pl.BlockSpec((n, block), lambda s, w, m: (0, s)) for n in rows],
            scratch_shapes=[
                pltpu.VMEM((holders, share, lanes), BF16),
                pltpu.VMEM((slab, lanes), F32),
                pltpu.SemaphoreType.DMA((holders,)),
            ]
            + [pltpu.VMEM((TILE, lanes), F32)] * run,
        ),
        out_shape=[jax.ShapeDtypeStruct((n, blocks * block), BF16) for n in rows],
        compiler_params=params(),
        cost_estimate=pl.CostEstimate(
            flops=(4 * sum(rows) * lanes + 40000) * blocks * block, bytes_accessed=1 * slab * lanes, transcendentals=0
        ),
        name="symmetrize",
    )(where, col_mirror, *parts)


def finish_kernel(cols, owned, half, run, turns, spans, where_ref, mirror_ref, slot_ref, *refs):
    count = len(spans)
    parts = refs[:count]
    out_ref, rows_ref, wide, sem, *picked = refs[count:]
    step = pl.program_id(0)
    slab, lanes = wide.shape
    pairs = out_ref.shape[0]
    sent = owned * half
    own = 2 * sent
    used = (cols - 1) * sent
    block = run * turns * TILE

    @pl.when(step == 0)
    def _():
        copies = []
        for m, (k, start, size) in enumerate(spans):
            at = pl.ds(own + (k - 1) * sent, sent) if k else pl.ds(0, own)
            copies.append(pltpu.make_async_copy(parts[m], rows_ref.at[at, pl.ds(start, size)], sem.at[m]))
        for copy in copies:
            copy.start()
        for copy in copies:
            copy.wait()

        def widen(n, carry):
            for i in range(run):
                at = pl.ds(pl.multiple_of((n * run + i) * TILE, TILE), TILE)
                rows = [rows_ref[own:, at].astype(F32)]
                if lanes > used:
                    rows.append(jnp.zeros((lanes - used, TILE), F32))
                wide[at, :] = jnp.concatenate(rows, axis=0).T
            return carry

        lax.fori_loop(0, slab // TILE // run, widen, 0)

    slot = jnp.broadcast_to(slot_ref[...], (pairs, pairs)).astype(F32).T.astype(I32)[:, :1]
    col = where_ref[1]
    onehots = [slot == col * own + iota((pairs, own), 1)]
    at = iota((pairs, used), 1)
    rest = at % sent
    first = (col ^ (at // sent + 1)) * own + (rest // half) * (2 * half) + rest % half
    onehots.append(slot == first)
    straight = jnp.concatenate([h.astype(F32) for h in onehots], axis=1).astype(BF16)
    second = [(slot == first + half).astype(F32)]
    if lanes > used:
        second.append(jnp.zeros((pairs, lanes - used), F32))
    crossed = jnp.concatenate(second, axis=1).astype(BF16)

    def some(n, carry):
        for i in range(run):
            inside = pl.multiple_of((n * run + i) * TILE, TILE)
            base = pl.multiple_of(step * block + inside, TILE)
            gather_rows(mirror_ref, base, wide, picked[i])
            total = lax.dot_general(straight, rows_ref[:, pl.ds(base, TILE)], NN, preferred_element_type=F32)
            total += lax.dot_general(crossed, picked[i][...].astype(BF16), NT, preferred_element_type=F32)
            out_ref[:, pl.ds(inside, TILE)] = total.astype(BF16)
        return carry

    lax.fori_loop(0, turns, some, 0)


def finish(where, col_mirror, slot, sums, spans, cols, owned, half):
    slab = col_mirror.shape[0]
    pairs = slot.shape[1]
    run, turns = runs_of(slab)
    block = run * turns * TILE
    lanes = pl.cdiv((cols - 1) * owned * half, 128) * 128
    return pl.pallas_call(
        functools.partial(finish_kernel, cols, owned, half, run, turns, spans),
        grid_spec=pltpu.PrefetchScalarGridSpec(
            num_scalar_prefetch=2,
            grid=(slab // block,),
            in_specs=[pl.BlockSpec((1, pairs), lambda s, w, m: (0, 0))]
            + [pl.BlockSpec(memory_space=pl.ANY)] * len(sums),
            out_specs=pl.BlockSpec((pairs, block), lambda s, w, m: (0, s)),
            scratch_shapes=[
                pltpu.VMEM(((cols + 1) * owned * half, slab), BF16),
                pltpu.VMEM((slab, lanes), F32),
                pltpu.SemaphoreType.DMA((len(sums),)),
            ]
            + [pltpu.VMEM((TILE, lanes), F32)] * run,
        ),
        out_shape=jax.ShapeDtypeStruct((pairs, slab), BF16),
        compiler_params=params(),
        cost_estimate=pl.CostEstimate(
            flops=2 * pairs * 256 * slab + 40000 * slab, bytes_accessed=8 * slab * lanes, transcendentals=0
        ),
        name="finish",
    )(where, col_mirror, slot, *sums)


def swap(array, axis, offset):
    return lax.ppermute(array, axis, [(i, i ^ offset) for i in range(lax.axis_size(axis))])


def after(arrays, earlier):
    earlier = tuple(earlier)
    return list(lax.optimization_barrier((tuple(arrays), earlier))[0]) if earlier else list(arrays)


def forward(held, order):
    reach = [0]
    fresh = []
    for bit in order:
        for offset in list(reach):
            if offset ^ bit not in held:
                held[offset ^ bit] = swap(held[offset], "row", bit)
                fresh.append(offset ^ bit)
            reach.append(offset ^ bit)
    return fresh


class Rows:
    def __init__(self):
        self.arrays, self.places = [], {}

    def add(self, keys, pieces):
        joined = jnp.concatenate(pieces) if len(pieces) > 1 else pieces[0]
        size = pieces[0].shape[0]
        for core, array in enumerate((joined, swap(joined, "row", 1))):
            for n, (offset, j) in enumerate(keys):
                self.places[offset ^ core, j] = (len(self.arrays), n * size)
            self.arrays.append(array)
        return self.arrays[-1]


def body(amplitudes, integrals, irreps, row_mirror, col_mirror):
    rows, cols = lax.axis_size("row"), lax.axis_size("col")
    owned = integrals.shape[0]
    pairs = amplitudes.shape[0]
    slots = pairs // 4
    half = slots // 2
    where = jnp.stack([lax.axis_index("row"), lax.axis_index("col")]).astype(I32)
    slot, packed = pack(where, irreps[None], row_mirror[None], amplitudes, cols, owned, half)
    outer = [1 << b for b in range(1, rows.bit_length() - 1)]
    combined = range(2, rows, 2)
    turns = max(1, cols // max(1, 4 // owned))
    batches = [tuple(range(first, cols, turns)) for first in range(turns)]
    integrals_t = jnp.swapaxes(integrals, 1, 2)

    ready = {}
    for k in range(cols):
        early = () if k < 3 else (ready[k - 1],)
        ready[k] = swap(after([packed[k]], early)[0], "col", k) if k else packed[0]

    parts = []
    for n, batch in enumerate(batches):
        gathered = Rows()
        held = []
        if n == 0:
            inner = []
            for j, k in enumerate(batch):
                (chunk,) = after([ready[k]], [ready[k - 1], *inner[:1]] if j else [])
                held = {0: chunk, **{o: swap(chunk, "row", o) for o in combined}}
                inner = [held[o] for o in combined[::-1]]
                if j == 0:
                    gathered.add([(o, j) for o in held], list(held.values()))
                    continue
                near, far = outer, [o for o in held if o not in outer]
                gathered.add([(o, j) for o in near], [held[o] for o in near])
                early = [ready[k + 1]] if k + 1 < cols else []
                gathered.add([(o, j) for o in far], after([held[o] for o in far], early))
        else:
            keys, pieces, fresh = [], [], []
            for j, k in enumerate(batch):
                held.append({0: ready[k], **{bit: swap(ready[k], "row", bit) for bit in outer}})
            for j, k in enumerate(batch):
                offsets = list(held[j])
                held[j] = dict(zip(offsets, after([held[j][o] for o in offsets], parts[-1][:1])))
                turn = j % len(outer)
                keys += [(o, j) for o in offsets]
                fresh += [(o, j) for o in forward(held[j], outer[turn:] + outer[:turn])]
            gathered.add(keys, [held[j][o] for o, j in keys])
            gathered.add(fresh, [held[j][o] for o, j in fresh])
        arrays = after(gathered.arrays, [part[1] for part in parts[-1:]])
        joined = n + 1 < turns
        part = list(product(arrays, gathered.places, integrals_t, rows, len(batch), slots, joined))
        if joined:
            part[1] = swap(part[1], "row", 1)
        parts.append(part)

    sums = {}
    results, totals, last, behind = (), (), (), []
    block = TILE * math.prod(runs_of(col_mirror.shape[0]))
    blocks = col_mirror.shape[0] // block
    cuts = []
    for n in range(turns):
        cut = (2 if n + 1 < turns else 3) * blocks // 5
        cuts.append([part for part in ((0, cut), (cut, blocks - cut)) if part[1]])
    for n, (batch, part) in enumerate(zip(batches, parts)):
        if n + 1 < turns:
            pieces = list(part)
            for o in combined:
                both = jnp.concatenate([array[o // 2 : o // 2 + 1] for array in part])
                pieces.append(swap(both, "row", o))
            last = pieces[2:]
            places = [(o, 0) if o < 2 else (o // 2 + 1, o % 2) for o in range(rows)]
        else:
            far = sorted(range(1, rows), key=lambda o: (-(o >> 1).bit_count(), -(o % 2), -o))
            pieces = list(part)
            for m, o in enumerate(far):
                early = last
                if m >= len(far) - 3:
                    early = [*results[:1], *(totals if m == len(far) - 1 else ())]
                pieces[o] = swap(after([pieces[o]], early)[0], "row", o)
            places = [(o, None) for o in range(rows)]
        results, totals = [], []
        for m, (first, count) in enumerate(cuts[n]):
            (turn,) = after([where], [*results[:1], *(behind if m else ())])
            results = symmetrize(turn, col_mirror, pieces, places, batch, owned, half, first, count)
            for k, total in zip(batch, results):
                sums[k, m] = total if k == 0 else swap(total, "col", k)
                if k and not m:
                    totals.append(sums[k, m])
        behind = [sums[k, len(cuts[n]) - 1] for k in batch if k]
    spans = {k: [(a * block, b * block) for a, b in cuts[n]] for n, batch in enumerate(batches) for k in batch}
    keys = sorted(sums)
    spans = [(k, *spans[k][m]) for k, m in keys]
    return finish(where, col_mirror, slot, [sums[key] for key in keys], spans, cols, owned, half)


def solution(mesh):
    return jax.shard_map(
        body,
        mesh=mesh,
        in_specs=(
            P(("row", "col"), None),
            P("col", None, "row"),
            P(("row", "col")),
            P(("row", "col")),
            P(),
        ),
        out_specs=P(("row", "col"), None),
        check_vma=False,
    )
```

```python
import functools
import math

import jax
import jax.numpy as jnp
from jax import lax
from jax.experimental import pallas as pl
from jax.experimental.pallas import tpu as pltpu
from jax.sharding import PartitionSpec as P

IRREPS = 8
F32, BF16, I32 = jnp.float32, jnp.bfloat16, jnp.int32
NN = (((1,), (0,)), ((), ()))
NT = (((1,), (1,)), ((), ()))
VMEM_LIMIT = 24 * 1024 * 1024
LADDER_LIMIT = 56 * 1024 * 1024
TILE = 128


def iota(shape, dim):
    return lax.broadcasted_iota(I32, shape, dim)


def params(limit=VMEM_LIMIT):
    return pltpu.CompilerParams(vmem_limit_bytes=limit)


def pack_kernel(cols, owned, half, where_ref, irreps_ref, mirror_ref, amp_ref, slot_ref, *out_refs):
    pairs = irreps_ref.shape[1]
    square = (pairs, pairs)
    irreps = jnp.broadcast_to(irreps_ref[...], square)
    mirror = jnp.broadcast_to(mirror_ref[...], square)
    irreps_t = irreps.astype(F32).T.astype(I32)
    mirror_t = mirror.astype(F32).T.astype(I32)
    down, across = iota(square, 0), iota(square, 1)
    first = jnp.minimum(across, mirror)
    counted = (mirror_t > down) & (irreps_t == irreps) & (down < first)
    rank = jnp.sum(counted.astype(I32), axis=0, keepdims=True)
    partner = (across[:1] != first[:1]).astype(I32)
    slot = irreps_ref[...] * (2 * half) + partner * half + rank
    slot_ref[...] = slot
    rows = owned * 2 * half
    amp = amp_ref[...]
    for k in range(cols):
        base = (where_ref[1] ^ k) * rows
        onehot = (slot == base + iota((rows, pairs), 0)).astype(F32).astype(BF16)
        out_refs[k][...] = lax.dot_general(onehot, amp, NN, preferred_element_type=F32).astype(BF16)


def pack(where, irreps, mirror, amplitudes, cols, owned, half):
    pairs, contract = amplitudes.shape
    rows = owned * 2 * half
    whole = lambda shape: pl.BlockSpec(shape, lambda i, w: (0, 0))
    out = pl.pallas_call(
        functools.partial(pack_kernel, cols, owned, half),
        grid_spec=pltpu.PrefetchScalarGridSpec(
            num_scalar_prefetch=1,
            grid=(1,),
            in_specs=[whole((1, pairs)), whole((1, pairs)), whole((pairs, contract))],
            out_specs=[whole((1, pairs))] + [whole((rows, contract))] * cols,
        ),
        out_shape=[jax.ShapeDtypeStruct((1, pairs), I32)]
        + [jax.ShapeDtypeStruct((rows, contract), BF16)] * cols,
        compiler_params=params(),
        cost_estimate=pl.CostEstimate(
            flops=2 * cols * rows * pairs * contract, bytes_accessed=3 * pairs * contract * 2, transcendentals=0
        ),
        name="pack",
    )(where, irreps, mirror, amplitudes)
    return out[0], out[1:]


def product_kernel(holders, chunk_count, owned, slots, places, array_count, *refs):
    arrays = refs[:array_count]
    integrals_ref, rows_ref, sem = refs[array_count], *refs[-2:]
    outs = refs[array_count + 1 : -2]
    group = chunk_count * slots

    @pl.when(pl.program_id(0) == 0)
    def _():
        copies = []
        for i in range(owned):
            for (o, j), (at, row) in places.items():
                n = len(copies)
                copies.append(
                    pltpu.make_async_copy(
                        arrays[at].at[pl.ds(row + i * slots, slots)],
                        rows_ref.at[i, pl.ds(o * group + j * slots, slots)],
                        sem.at[n],
                    )
                )
        for copy in copies:
            copy.start()
        for copy in copies:
            copy.wait()

    ladder = [
        lax.dot_general(integrals_ref[i], rows_ref[i], NT, preferred_element_type=F32) for i in range(owned)
    ]
    for o in range(holders):
        here = slice(o * group, (o + 1) * group)
        block = jnp.concatenate([ladder[i][:, here] for i in range(owned)], axis=1).astype(BF16)
        if len(outs) == 2:
            outs[o % 2][o // 2] = block
        else:
            outs[o][...] = block


def product(arrays, places, integrals, holders, chunk_count, slots, joined):
    owned, share, contract = integrals.shape
    tile = 240
    group = chunk_count * slots
    lanes = owned * group
    if joined:
        spec = pl.BlockSpec((holders // 2, tile, lanes), lambda s: (0, s, 0))
        out = jax.ShapeDtypeStruct((holders // 2, share, lanes), BF16)
    else:
        spec = pl.BlockSpec((tile, lanes), lambda s: (s, 0))
        out = jax.ShapeDtypeStruct((share, lanes), BF16)
    return pl.pallas_call(
        functools.partial(product_kernel, holders, chunk_count, owned, slots, places, len(arrays)),
        grid=(pl.cdiv(share, tile),),
        in_specs=[pl.BlockSpec(memory_space=pl.ANY)] * len(arrays)
        + [pl.BlockSpec((owned, tile, contract), lambda s: (0, s, 0))],
        out_specs=[spec] * (2 if joined else holders),
        out_shape=[out] * (2 if joined else holders),
        scratch_shapes=[
            pltpu.VMEM((owned, holders * group, contract), BF16),
            pltpu.SemaphoreType.DMA((holders * chunk_count * owned,)),
        ],
        compiler_params=params(LADDER_LIMIT),
        cost_estimate=pl.CostEstimate(
            flops=2 * owned * holders * group * contract * share,
            bytes_accessed=2 * owned * contract * (share + holders * group),
            transcendentals=0,
        ),
        name="ladder",
    )(*arrays, integrals)


def gather_rows(mirror_ref, base, source, target):
    rows = [source[pl.ds(mirror_ref[base + u], 1), :] for u in range(target.shape[0])]
    for u, row in enumerate(rows):
        target[u : u + 1, :] = row


def runs_of(slab):
    tiles = slab // TILE
    return next(n for n in (15, 5, 3, 4, 2, 1) if tiles % n == 0), 1


def symmetrize_kernel(places, array_count, chunks, owned, half, run, turns, offset, where_ref, mirror_ref, *refs):
    holders = len(places)
    parts, refs = refs[:array_count], refs[array_count:]
    outs, refs = refs[: len(chunks)], refs[len(chunks) :]
    raw, wide, sem, *picked = refs
    share, lanes = raw.shape[1:]
    step = pl.program_id(0)

    @pl.when(step == 0)
    def _():
        copies = []
        for o in range(holders):
            at, index = places[o]
            part = parts[at] if index is None else parts[at].at[index]
            copies.append(pltpu.make_async_copy(part, raw.at[o], sem.at[o]))
        for copy in copies:
            copy.start()
        for o in range(holders):
            copies[o].wait()
            at = pl.multiple_of((where_ref[0] ^ o) * share, 8)
            wide[pl.ds(at, share), :] = raw[o].astype(F32)

    group = len(chunks) * 2 * half
    picks = []
    for j, k in enumerate(chunks):
        sides = 2 if k == 0 else 1
        shape = (outs[j].shape[0], lanes)
        row, lane = iota(shape, 0), iota(shape, 1)
        irrep, rest = row // (sides * half), row % (sides * half)
        side, rank = rest // half, rest % half
        start = irrep * group + j * 2 * half + rank
        mine = lane == start + side * half
        other = lane == start + (1 - side) * half
        picks.append(jnp.concatenate([mine.astype(F32), other.astype(F32)], axis=1))
    pick = jnp.concatenate(picks, axis=0).astype(BF16)

    def some(n, carry):
        for i in range(run):
            inside = pl.multiple_of((n * run + i) * TILE, TILE)
            base = (step + offset) * (turns * run * TILE) + inside
            gather_rows(mirror_ref, base, wide, picked[i])
            here = wide[pl.ds(pl.multiple_of(base, TILE), TILE), :]
            both = jnp.concatenate([here, picked[i][...]], axis=1).astype(BF16)
            total = lax.dot_general(pick, both, NT, preferred_element_type=F32).astype(BF16)
            at = 0
            for out in outs:
                out[:, pl.ds(inside, TILE)] = total[at : at + out.shape[0]]
                at += out.shape[0]
        return carry

    lax.fori_loop(0, turns, some, 0)


def symmetrize(where, col_mirror, parts, places, chunks, owned, half, first, blocks):
    holders = len(places)
    share, lanes = parts[0].shape[-2:]
    slab = col_mirror.shape[0]
    run, turns = runs_of(slab)
    block = run * turns * TILE
    rows = [owned * half * (2 if k == 0 else 1) for k in chunks]
    return pl.pallas_call(
        functools.partial(symmetrize_kernel, places, len(parts), chunks, owned, half, run, turns, first),
        grid_spec=pltpu.PrefetchScalarGridSpec(
            num_scalar_prefetch=2,
            grid=(blocks,),
            in_specs=[pl.BlockSpec(memory_space=pl.ANY)] * len(parts),
            out_specs=[pl.BlockSpec((n, block), lambda s, w, m: (0, s)) for n in rows],
            scratch_shapes=[
                pltpu.VMEM((holders, share, lanes), BF16),
                pltpu.VMEM((slab, lanes), F32),
                pltpu.SemaphoreType.DMA((holders,)),
            ]
            + [pltpu.VMEM((TILE, lanes), F32)] * run,
        ),
        out_shape=[jax.ShapeDtypeStruct((n, blocks * block), BF16) for n in rows],
        compiler_params=params(),
        cost_estimate=pl.CostEstimate(
            flops=(4 * sum(rows) * lanes + 40000) * blocks * block, bytes_accessed=1 * slab * lanes, transcendentals=0
        ),
        name="symmetrize",
    )(where, col_mirror, *parts)


def finish_kernel(cols, owned, half, run, turns, spans, where_ref, mirror_ref, slot_ref, *refs):
    count = len(spans)
    parts = refs[:count]
    out_ref, rows_ref, wide, sem, *picked = refs[count:]
    step = pl.program_id(0)
    slab, lanes = wide.shape
    pairs = out_ref.shape[0]
    sent = owned * half
    own = 2 * sent
    used = (cols - 1) * sent
    block = run * turns * TILE

    @pl.when(step == 0)
    def _():
        copies = []
        for m, (k, start, size) in enumerate(spans):
            at = pl.ds(own + (k - 1) * sent, sent) if k else pl.ds(0, own)
            copies.append(pltpu.make_async_copy(parts[m], rows_ref.at[at, pl.ds(start, size)], sem.at[m]))
        for copy in copies:
            copy.start()
        for copy in copies:
            copy.wait()

        def widen(n, carry):
            for i in range(run):
                at = pl.ds(pl.multiple_of((n * run + i) * TILE, TILE), TILE)
                rows = [rows_ref[own:, at].astype(F32)]
                if lanes > used:
                    rows.append(jnp.zeros((lanes - used, TILE), F32))
                wide[at, :] = jnp.concatenate(rows, axis=0).T
            return carry

        lax.fori_loop(0, slab // TILE // run, widen, 0)

    slot = jnp.broadcast_to(slot_ref[...], (pairs, pairs)).astype(F32).T.astype(I32)[:, :1]
    col = where_ref[1]
    onehots = [slot == col * own + iota((pairs, own), 1)]
    at = iota((pairs, used), 1)
    rest = at % sent
    first = (col ^ (at // sent + 1)) * own + (rest // half) * (2 * half) + rest % half
    onehots.append(slot == first)
    straight = jnp.concatenate([h.astype(F32) for h in onehots], axis=1).astype(BF16)
    second = [(slot == first + half).astype(F32)]
    if lanes > used:
        second.append(jnp.zeros((pairs, lanes - used), F32))
    crossed = jnp.concatenate(second, axis=1).astype(BF16)

    def some(n, carry):
        for i in range(run):
            inside = pl.multiple_of((n * run + i) * TILE, TILE)
            base = pl.multiple_of(step * block + inside, TILE)
            gather_rows(mirror_ref, base, wide, picked[i])
            total = lax.dot_general(straight, rows_ref[:, pl.ds(base, TILE)], NN, preferred_element_type=F32)
            total += lax.dot_general(crossed, picked[i][...].astype(BF16), NT, preferred_element_type=F32)
            out_ref[:, pl.ds(inside, TILE)] = total.astype(BF16)
        return carry

    lax.fori_loop(0, turns, some, 0)


def finish(where, col_mirror, slot, sums, spans, cols, owned, half):
    slab = col_mirror.shape[0]
    pairs = slot.shape[1]
    run, turns = runs_of(slab)
    block = run * turns * TILE
    lanes = pl.cdiv((cols - 1) * owned * half, 128) * 128
    return pl.pallas_call(
        functools.partial(finish_kernel, cols, owned, half, run, turns, spans),
        grid_spec=pltpu.PrefetchScalarGridSpec(
            num_scalar_prefetch=2,
            grid=(slab // block,),
            in_specs=[pl.BlockSpec((1, pairs), lambda s, w, m: (0, 0))]
            + [pl.BlockSpec(memory_space=pl.ANY)] * len(sums),
            out_specs=pl.BlockSpec((pairs, block), lambda s, w, m: (0, s)),
            scratch_shapes=[
                pltpu.VMEM(((cols + 1) * owned * half, slab), BF16),
                pltpu.VMEM((slab, lanes), F32),
                pltpu.SemaphoreType.DMA((len(sums),)),
            ]
            + [pltpu.VMEM((TILE, lanes), F32)] * run,
        ),
        out_shape=jax.ShapeDtypeStruct((pairs, slab), BF16),
        compiler_params=params(),
        cost_estimate=pl.CostEstimate(
            flops=2 * pairs * 256 * slab + 40000 * slab, bytes_accessed=8 * slab * lanes, transcendentals=0
        ),
        name="finish",
    )(where, col_mirror, slot, *sums)


def swap(array, axis, offset):
    return lax.ppermute(array, axis, [(i, i ^ offset) for i in range(lax.axis_size(axis))])


def after(arrays, earlier):
    earlier = tuple(earlier)
    return list(lax.optimization_barrier((tuple(arrays), earlier))[0]) if earlier else list(arrays)


def forward(held, order):
    reach = [0]
    fresh = []
    for bit in order:
        for offset in list(reach):
            if offset ^ bit not in held:
                held[offset ^ bit] = swap(held[offset], "row", bit)
                fresh.append(offset ^ bit)
            reach.append(offset ^ bit)
    return fresh


class Rows:
    def __init__(self):
        self.arrays, self.places = [], {}

    def add(self, keys, pieces):
        joined = jnp.concatenate(pieces) if len(pieces) > 1 else pieces[0]
        size = pieces[0].shape[0]
        for core, array in enumerate((joined, swap(joined, "row", 1))):
            for n, (offset, j) in enumerate(keys):
                self.places[offset ^ core, j] = (len(self.arrays), n * size)
            self.arrays.append(array)
        return self.arrays[-1]


def body(amplitudes, integrals, irreps, row_mirror, col_mirror):
    rows, cols = lax.axis_size("row"), lax.axis_size("col")
    owned = integrals.shape[0]
    pairs = amplitudes.shape[0]
    slots = pairs // 4
    half = slots // 2
    where = jnp.stack([lax.axis_index("row"), lax.axis_index("col")]).astype(I32)
    slot, packed = pack(where, irreps[None], row_mirror[None], amplitudes, cols, owned, half)
    outer = [1 << b for b in range(1, rows.bit_length() - 1)]
    combined = range(2, rows, 2)
    turns = max(1, cols // max(1, 4 // owned))
    batches = [tuple(range(first, cols, turns)) for first in range(turns)]
    integrals_t = jnp.swapaxes(integrals, 1, 2)

    ready = {}
    for k in range(cols):
        early = () if k < 3 else (ready[k - 1],)
        ready[k] = swap(after([packed[k]], early)[0], "col", k) if k else packed[0]

    parts = []
    for n, batch in enumerate(batches):
        gathered = Rows()
        held = []
        if n == 0:
            inner = []
            for j, k in enumerate(batch):
                (chunk,) = after([ready[k]], [ready[k - 1], *inner[:1]] if j else [])
                held = {0: chunk, **{o: swap(chunk, "row", o) for o in combined}}
                inner = [held[o] for o in combined[::-1]]
                if j == 0:
                    gathered.add([(o, j) for o in held], list(held.values()))
                    continue
                near, far = outer, [o for o in held if o not in outer]
                gathered.add([(o, j) for o in near], [held[o] for o in near])
                early = [ready[k + 1]] if k + 1 < cols else []
                gathered.add([(o, j) for o in far], after([held[o] for o in far], early))
        else:
            keys, pieces, fresh = [], [], []
            for j, k in enumerate(batch):
                held.append({0: ready[k], **{bit: swap(ready[k], "row", bit) for bit in outer}})
            for j, k in enumerate(batch):
                offsets = list(held[j])
                held[j] = dict(zip(offsets, after([held[j][o] for o in offsets], parts[-1][:1])))
                turn = j % len(outer)
                keys += [(o, j) for o in offsets]
                fresh += [(o, j) for o in forward(held[j], outer[turn:] + outer[:turn])]
            gathered.add(keys, [held[j][o] for o, j in keys])
            gathered.add(fresh, [held[j][o] for o, j in fresh])
        arrays = after(gathered.arrays, [part[1] for part in parts[-1:]])
        joined = n + 1 < turns
        part = list(product(arrays, gathered.places, integrals_t, rows, len(batch), slots, joined))
        if joined:
            part[1] = swap(part[1], "row", 1)
        parts.append(part)

    sums = {}
    results, totals, last, behind = (), (), (), []
    block = TILE * math.prod(runs_of(col_mirror.shape[0]))
    blocks = col_mirror.shape[0] // block
    cuts = []
    for n in range(turns):
        cut = (2 if n + 1 < turns else 3) * blocks // 5
        cuts.append([part for part in ((0, cut), (cut, blocks - cut)) if part[1]])
    for n, (batch, part) in enumerate(zip(batches, parts)):
        if n + 1 < turns:
            pieces = list(part)
            for o in combined:
                both = jnp.concatenate([array[o // 2 : o // 2 + 1] for array in part])
                pieces.append(swap(both, "row", o))
            last = pieces[2:]
            places = [(o, 0) if o < 2 else (o // 2 + 1, o % 2) for o in range(rows)]
        else:
            far = sorted(range(1, rows), key=lambda o: (-(o >> 1).bit_count(), -(o % 2), -o))
            pieces = list(part)
            for m, o in enumerate(far):
                early = last[-1:]
                if m >= len(far) - 3:
                    early = [*results[:1], *(totals if m == len(far) - 1 else ())]
                pieces[o] = swap(after([pieces[o]], early)[0], "row", o)
            places = [(o, None) for o in range(rows)]
        results, totals = [], []
        for m, (first, count) in enumerate(cuts[n]):
            (turn,) = after([where], [*results[:1], *(behind if m else ())])
            results = symmetrize(turn, col_mirror, pieces, places, batch, owned, half, first, count)
            for k, total in zip(batch, results):
                sums[k, m] = total if k == 0 else swap(total, "col", k)
                if k and not m:
                    totals.append(sums[k, m])
        behind = [sums[k, len(cuts[n]) - 1] for k in batch if k]
    spans = {k: [(a * block, b * block) for a, b in cuts[n]] for n, batch in enumerate(batches) for k in batch}
    keys = sorted(sums)
    spans = [(k, *spans[k][m]) for k, m in keys]
    return finish(where, col_mirror, slot, [sums[key] for key in keys], spans, cols, owned, half)


def solution(mesh):
    return jax.shard_map(
        body,
        mesh=mesh,
        in_specs=(
            P(("row", "col"), None),
            P("col", None, "row"),
            P(("row", "col")),
            P(("row", "col")),
            P(),
        ),
        out_specs=P(("row", "col"), None),
        check_vma=False,
    )
```
